32 devices in a mesh: dp: 4 (over y, x), expert: 8 (over z, core).
Axes of the slice: x: 2, y: 2, z: 4, core: 2. Of those that a mesh axis runs over, the one named last changes fastest.
Arguments:
- tokens: bfloat16 [32768, 768], P(('dp', 'expert')), may hold values from -6 to 6
- cotangent: bfloat16 [32768, 768], P(('dp', 'expert')), may hold values from -6 to 6
- lengths: int32 [64, 3], P(('dp', 'expert')), may hold values from 1 to 384, 512 in all within a row
- routes: int32 [32768, 1], P(('dp', 'expert')), may hold values from 0 to 15; in each aligned block of 512 rows (0 to 511, 512 to 1023, ...) at most 64 rows name the same one
- w_query: bfloat16 [768, 768], P(('dp', 'expert')), may hold values from -0.21875 to 0.21875
- w_key: bfloat16 [768, 768], P(('dp', 'expert')), may hold values from -0.21875 to 0.21875
- w_value: bfloat16 [768, 768], P(('dp', 'expert')), may hold values from -0.21875 to 0.21875
- w_output: bfloat16 [768, 768], P(('dp', 'expert')), may hold values from -1.25 to 1.25
- router: bfloat16 [768, 16], P(('dp', 'expert')), may hold values from -0.109375 to 0.109375
- gain_first: bfloat16 [768], P(('dp', 'expert')), may hold values from 0.5 to 1.5
- gain_second: bfloat16 [768], P(('dp', 'expert')), may hold values from 0.5 to 1.5
- bias_table: float32 [32, 12], replicated, may hold values from -4 to 4
- w_in: bfloat16 [16, 768, 3072], P('expert', None, 'dp'), may hold values from -0.21875 to 0.21875
- w_out: bfloat16 [16, 3072, 768], P('expert', 'dp')
Outputs:
- block_out: bfloat16 [32768, 768], P(('dp', 'expert'))
- grad_tokens: float32 [32768, 768], P(('dp', 'expert'))
- grad_query: float32 [768, 768], P(('dp', 'expert'))
- grad_key: float32 [768, 768], P(('dp', 'expert'))
- grad_value: float32 [768, 768], P(('dp', 'expert'))
- grad_output: float32 [768, 768], P(('dp', 'expert'))
- grad_router: float32 [768, 16], P(('dp', 'expert'))
- grad_gain_first: float32 [768], P(('dp', 'expert'))
- grad_gain_second: float32 [768], P(('dp', 'expert'))
- grad_bias_table: float32 [32, 12], replicated
- grad_in: float32 [16, 768, 3072], P('expert', None, 'dp')
- grad_out: float32 [16, 3072, 768], P('expert', 'dp')
The draws below stay inside these ranges and needn't reach their ends.
Inputs may be any that keep to these rules, and one draw needn't show every extreme that they name: Each row holds the lengths of the sequences of one micro-batch block, in order; they sum to 512. `routes`: within each micro-batch block (8 on the larger slice: 2 * 512 / experts) of 512 rows of one device, no expert is named by more than 64 tokens.
All inputs are finite; a program needn't handle non-finite values.
Results may differ from the reference program's by a relative error of at most 0.023.
Values may be sent and summed in bfloat16 or wider, within the bound.
A program may use at most 320 MiB of HBM per device.

```python
import math
import jax
import jax.numpy as jnp
import numpy as np
from jax import lax

D = 768
H = 12
HD = 64
FF = 3072
NB = 32
MB_TOK = 512
NSEQ = 3
SEQMAX = 384
EXPERTS = 16
TOKENS = 32768
BLOCKS = 64
CAP = 64
N_DP = 4


def draw_w_out(key, part):
    key = jax.random.fold_in(key, 11)
    values = jax.random.truncated_normal(key, -4.0, 4.0, (EXPERTS, FF, D), jnp.float32)
    return (values * (2.0 * EXPERTS / math.sqrt(FF))).astype(jnp.bfloat16)


def steps_of(own_key, shape, split, smallest, high):
    def one(position, shards_of):
        draws = jax.random.uniform(jax.random.fold_in(jax.random.fold_in(own_key, 6), position), (shards_of,), jnp.float32, smallest / len(split), high / len(split))
        return jnp.repeat(jnp.exp(draws), shape[position] // shards_of).reshape((-1,) + (1,) * (len(shape) - position - 1))

    gain = one(*split[0])
    for cut in split[1:]:
        gain = gain * one(*cut)
    return gain


def split_up(count, total, reach, skew):
    weights = [(1 << 20) // math.isqrt(rank ** skew) + 1 for rank in range(2, count + 1)]
    spare, given = total - reach - (count - 1), [1] * (count - 1)
    while spare > 0:
        free = [i for i in range(count - 1) if given[i] < reach]
        mass, remaining = sum([weights[i] for i in free]), spare
        for i in free:
            extra = min(reach - given[i], max(1, remaining * weights[i] // mass), spare)
            given[i] = given[i] + extra
            spare = spare - extra
    return np.array([reach] + given)


def ragged_sizes(rng, count, total, reach, lean):
    if count == 2:
        one = jax.random.randint(rng, (), max(1, total - reach), min(reach, total - 1) + 1)
        return jnp.stack([one, total - one])
    sizes = jnp.asarray(split_up(count, total, reach, lean), jnp.int32)
    twos = (count - 1) // 2
    source_of, sink = sizes[1:1 + 2 * twos:2], sizes[2:2 + 2 * twos:2]
    room = jnp.minimum(source_of - 1, reach - sink)
    moved = jax.random.randint(jax.random.fold_in(rng, 1), (twos,), 0, 1 << 20) % (room + 1)
    sizes = sizes.at[1:1 + 2 * twos:2].set(source_of - moved).at[2:2 + 2 * twos:2].set(sink + moved)
    return sizes[jax.random.permutation(jax.random.fold_in(rng, 2), count)]


def routed_block(key, own, number, rows, number_of, top, bound, skew):
    ranking = jax.random.permutation(key, number_of)
    heavy_load, common = load_shares(number_of, rows * top, bound, skew, True), load_shares(number_of, rows * top, bound, skew, False)
    places = jnp.arange(number_of)

    def named(sizes, offset_by):
        used = int((sizes > 0).sum())
        fixed = max(1, used // 4)
        moved = fixed + (places - fixed + offset_by * (used - fixed)) % max(1, number_of - fixed)
        return jnp.zeros((number_of,), jnp.int32).at[ranking[jnp.where(places < fixed, places, moved)]].set(jnp.asarray(sizes, jnp.int32))

    sizes = jnp.where(number % 4 == 0, named(heavy_load, number // 4), named(common, number - number // 4 - 1))
    mixed = jax.random.permutation(jax.random.fold_in(own, 3), number_of)
    giver, sink = mixed[0:number_of // 2 * 2:2], mixed[1:number_of // 2 * 2:2]
    slack = jnp.minimum(sizes[giver] - 1, bound - sizes[sink]) // 2
    slack = jnp.where((giver == ranking[0]) | (sink == ranking[0]) | (sizes[sink] == 0), 0, jnp.maximum(slack, 0))
    moved = jax.random.randint(jax.random.fold_in(own, 4), (number_of // 2,), 0, 1 << 20) % (slack + 1)
    sizes = sizes.at[giver].add(-moved).at[sink].add(moved)
    labels = jnp.searchsorted(jnp.cumsum(sizes), jnp.arange(rows * top), side="right").astype(jnp.int32)
    grid = labels.reshape(top, rows).T
    grid = grid[jax.random.permutation(jax.random.fold_in(own, 1), rows)]
    offset_by = jax.random.randint(jax.random.fold_in(own, 2), (rows, 1), 0, top)
    return jnp.take_along_axis(grid, (jnp.arange(top)[None, :] + offset_by) % top, axis=1)


def load_shares(count, total, most, lean, full):
    loads = [(1 << 20) // math.isqrt(standing ** lean) + 1 for standing in range(1, count + 1)]
    largest = most if full else min(most, max(-(-total // count), total * loads[0] // sum(loads)))
    least = 1 if total - largest >= count - 1 else 0
    counts, rest = [largest] + [least] * (count - 1), total - largest - least * (count - 1)
    while rest > 0:
        movable = [i for i in range(1, count) if counts[i] < largest] or [i for i in range(1, count) if counts[i] < most]
        mass, left = sum([loads[i] for i in movable]), rest
        for i in movable:
            addition = min(most - counts[i], max(1, left * loads[i] // mass), rest)
            counts[i] = counts[i] + addition
            rest = rest - addition
    return np.array(counts)


def centred(own_key, dims, width, limit, shards=(), kind=jnp.bfloat16):
    entries = width * jax.random.normal(own_key, dims, jnp.float32)
    if shards:
        entries = entries * steps_of(own_key, dims, shards, -0.22, 0.18)
    return jnp.clip(entries, -limit, limit).astype(kind)


def setup_inputs(seed: int = 0) -> dict:
    keys = jax.random.split(jax.random.key(seed), 15)
    tokens = centred(keys[0], (TOKENS, D), 1.0, 6.0, ((0, 32),))
    cotangent = centred(keys[1], (TOKENS, D), 1.0, 6.0, ((0, 32),))
    lengths = jax.vmap(lambda own: ragged_sizes(own, NSEQ, MB_TOK, SEQMAX, 2))(jax.random.split(keys[2], BLOCKS)).reshape((BLOCKS, NSEQ)).astype(jnp.int32)
    routes_keys = jax.random.split(jax.random.fold_in(keys[3], 1), TOKENS // MB_TOK)
    routes_turns = jax.random.permutation(jax.random.fold_in(keys[3], 3), TOKENS // MB_TOK)
    routes = jax.vmap(lambda own, number: routed_block(jax.random.fold_in(keys[3], 2), own, number, MB_TOK, EXPERTS, 1, CAP, 1))(routes_keys, routes_turns).reshape((TOKENS, 1))
    w_query = centred(keys[4], (D, D), D ** -0.5, 0.21875, ((0, 32),))
    w_key = centred(keys[5], (D, D), D ** -0.5, 0.21875, ((0, 32),))
    w_value = centred(keys[6], (D, D), D ** -0.5, 0.21875, ((0, 32),))
    w_output = centred(keys[7], (D, D), (D // 32) ** -0.5, 1.25, ((0, 32),))
    router = centred(keys[8], (D, EXPERTS), (4 * D) ** -0.5, 0.109375, ((0, 32),))
    gain_first = jnp.clip(1.0 + 0.1 * jax.random.normal(keys[9], (D,), jnp.float32), 0.5, 1.5).astype(jnp.bfloat16)
    gain_second = jnp.clip(1.0 + 0.1 * jax.random.normal(keys[10], (D,), jnp.float32), 0.5, 1.5).astype(jnp.bfloat16)
    bias_table = centred(keys[11], (NB, H), 0.7, 4.0, (), jnp.float32)
    w_in = centred(keys[12], (EXPERTS, D, FF), D ** -0.5, 0.21875, ((0, 8), (2, 4)))
    w_out = draw_w_out(jax.random.fold_in(keys[14], 71), 0)
    return dict(tokens=tokens, cotangent=cotangent, lengths=lengths, routes=routes, w_query=w_query, w_key=w_key, w_value=w_value, w_output=w_output, router=router, gain_first=gain_first, gain_second=gain_second, bias_table=bias_table, w_in=w_in, w_out=w_out)


EPSILON = 1e-06
THRESHOLDS = (12, 16, 23, 32, 46, 64, 91)
NEGATIVE = -1e+30

@jax.custom_vjp
def low(v):
    return lax.optimization_barrier(v.astype(jnp.bfloat16)).astype(jnp.float32)

@jax.custom_vjp
def low_back(v):
    return v

def low_keep(v):
    return (low(v), None)

def low_pass(kept, grad):
    return (grad,)

def back_keep(v):
    return (v, None)

def back_low(kept, grad):
    return (low(grad),)
low.defvjp(low_keep, low_pass)
low_back.defvjp(back_keep, back_low)

def matmul(former, latter):
    return jnp.dot(former, latter, precision=lax.Precision.HIGHEST, preferred_element_type=jnp.float32)

def rms_scaled(values, gain_vector):
    return values * lax.rsqrt(lax.optimization_barrier(jnp.mean(values * values, axis=-1, keepdims=True)) + EPSILON) * gain_vector

def gelu_tanh(values):
    return jax.nn.gelu(values, approximate=True)

def bucket_grid(extent):
    places = jnp.arange(extent, dtype=jnp.int32)
    offset = places[None, :] - places[:, None]
    spread = jnp.abs(offset)
    beyond = 8 + sum(((spread >= threshold).astype(jnp.int32) for threshold in THRESHOLDS))
    return jnp.where(offset > 0, 16, 0).astype(jnp.int32) + jnp.where(spread < 8, spread, beyond).astype(jnp.int32)

def same_sequence(seq_lengths, extent):
    places = jnp.arange(extent, dtype=jnp.int32)
    ending = jnp.cumsum(seq_lengths).astype(jnp.int32)
    segment = lax.optimization_barrier(jnp.sum((places[:, None] >= ending[None, :]).astype(jnp.int32), axis=1))
    return segment[:, None] == segment[None, :]

def attend(normed_block, seq_lengths, w_query, w_key, w_value, w_output, bias_grid):
    query_rows = low(low_back(matmul(normed_block, w_query))).reshape(MB_TOK, H, HD)
    keys_block = low(low_back(matmul(normed_block, w_key))).reshape(MB_TOK, H, HD)
    values_block = low(low_back(matmul(normed_block, w_value))).reshape(MB_TOK, H, HD)
    scores = jnp.einsum('phd,qhd->hpq', query_rows, keys_block, precision=lax.Precision.HIGHEST) * HD ** (-0.5)
    scores = low_back(scores + bias_grid)
    allowed = same_sequence(seq_lengths, MB_TOK)
    masked = jnp.where(allowed[None], scores, NEGATIVE)
    row_peak = lax.optimization_barrier(jnp.max(masked, axis=-1, keepdims=True))
    exps = jnp.exp(masked - row_peak)
    soft_weights = low(exps / lax.optimization_barrier(jnp.sum(exps, axis=-1, keepdims=True)))
    context = jnp.einsum('hpq,qhd->phd', soft_weights, values_block, precision=lax.Precision.HIGHEST)
    context = low(low_back(context.reshape(MB_TOK, H * HD)))
    return low_back(matmul(context, w_output))

def expert_apply(items):
    expert_rows, in_weight, out_weight = items
    group_width = FF // N_DP
    expert_sum = jnp.zeros((expert_rows.shape[0], D), jnp.float32)
    for quarter in range(N_DP):
        rows_copy = low_back(expert_rows)
        expert_pre = low_back(matmul(rows_copy, in_weight[:, quarter * group_width:(quarter + 1) * group_width]))
        hidden = low(gelu_tanh(expert_pre))
        expert_sum = expert_sum + low(matmul(hidden, out_weight[quarter * group_width:(quarter + 1) * group_width]))
    return expert_sum

def reference(tokens, cotangent, lengths, routes, w_query, w_key, w_value, w_output, router, gain_first, gain_second, bias_table, w_in, w_out):
    route_flat = routes[:, 0].astype(jnp.int32)
    choose = (route_flat.reshape(BLOCKS, MB_TOK)[:, :, None] == jnp.arange(EXPERTS, dtype=jnp.int32)[None, None, :]).astype(jnp.int32)
    slot_index = (lax.optimization_barrier(jnp.sum(jnp.cumsum(choose, axis=1) * choose, axis=-1)) - 1).reshape(TOKENS)
    block_id = (jnp.arange(TOKENS, dtype=jnp.int32) // MB_TOK).astype(jnp.int32)
    row_index = (route_flat * (BLOCKS * CAP) + block_id * CAP + slot_index).astype(jnp.int32)
    bucket = bucket_grid(MB_TOK)

    def forward(tokens_f, query_w, key_w, value_w, output_w, router_w, first_gain, second_gain, table_f, in_w, out_w):
        normed = low(rms_scaled(tokens_f, first_gain))
        bias_grid = jnp.moveaxis(table_f[bucket], 2, 0)

        def block_step(items):
            return attend(items[0], items[1], query_w, key_w, value_w, output_w, bias_grid)
        attended = lax.map(jax.checkpoint(block_step), (normed.reshape(BLOCKS, MB_TOK, D), lengths))
        middle = tokens_f + attended.reshape(TOKENS, D)
        second = low(rms_scaled(middle, second_gain))
        logits = low_back(matmul(second, router_w))
        row_peak = lax.optimization_barrier(jnp.max(logits, axis=-1, keepdims=True))
        exps = jnp.exp(logits - row_peak)
        gate_probs = exps / lax.optimization_barrier(jnp.sum(exps, axis=-1, keepdims=True))
        gate_value = jnp.take_along_axis(gate_probs, route_flat[:, None], axis=1)[:, 0]
        buffer = jnp.zeros((EXPERTS * BLOCKS * CAP, D), jnp.float32).at[row_index].set(second)
        buffer = low_back(buffer).reshape(EXPERTS, BLOCKS * CAP, D)
        expert_sum = lax.map(jax.checkpoint(expert_apply), (buffer, in_w, out_w))
        expert_rows = low(low_back(expert_sum)).reshape(EXPERTS * BLOCKS * CAP, D)
        return middle + gate_value[:, None] * expert_rows[row_index]
    floats = tuple((member.astype(jnp.float32) for member in (tokens, w_query, w_key, w_value, w_output, router, gain_first, gain_second, bias_table, w_in, w_out)))
    result, pullback = jax.vjp(forward, *floats)
    grads = pullback(cotangent.astype(jnp.float32))
    return (result.astype(jnp.bfloat16), grads[0], grads[1], grads[2], grads[3], grads[4], grads[5], grads[6], grads[7], grads[8], grads[9], grads[10])
```

```python
import jax
import jax.numpy as jnp
from jax import lax
from jax.sharding import PartitionSpec as P

H = 12
HD = 64


EPSILON = 1e-06
THRESHOLDS = (12, 16, 23, 32, 46, 64, 91)
NEGATIVE = -1e30


def bucket_grid(extent):
    places = jnp.arange(extent, dtype=jnp.int32)
    offset = places[None, :] - places[:, None]
    spread = jnp.abs(offset)
    beyond = 8 + sum(((spread >= threshold).astype(jnp.int32) for threshold in THRESHOLDS))
    return jnp.where(offset > 0, 16, 0).astype(jnp.int32) + jnp.where(spread < 8, spread, beyond)


def same_sequence(seq_lengths, extent):
    places = jnp.arange(extent, dtype=jnp.int32)
    ending = jnp.cumsum(seq_lengths)
    segment = jnp.sum((places[:, None] >= ending[None, :]).astype(jnp.int32), axis=1)
    return segment[:, None] == segment[None, :]


def gelu_tanh(values):
    return jax.nn.gelu(values, approximate=True)


def rms_forward(values, gain_vector):
    scale_row = lax.rsqrt(jnp.mean(values * values, axis=-1, keepdims=True) + EPSILON)
    return (scale_row, values * scale_row * gain_vector)


def rms_backward(values, scale_row, gain_vector, grad_scaled):
    weighted = grad_scaled * gain_vector
    grad_values = scale_row * weighted - values * scale_row**3 * jnp.mean(
        weighted * values, axis=-1, keepdims=True
    )
    grad_gain = jnp.sum(grad_scaled * values * scale_row, axis=0)
    return (grad_values, grad_gain)


def contract_rows(former, latter):
    return lax.dot_general(
        former, latter, (((0,), (0,)), ((), ())), preferred_element_type=jnp.float32
    )


def contract_cols(former, latter):
    return lax.dot_general(
        former, latter, (((1,), (1,)), ((), ())), preferred_element_type=jnp.float32
    )


def attention_scores(query, key, bias_grid, allowed):
    scores = jnp.einsum("bphd,bqhd->bhpq", query, key, preferred_element_type=jnp.float32)
    return jnp.where(allowed[:, None], scores * HD ** (-0.5) + bias_grid[None], NEGATIVE)


def sum_everywhere(values, axes):
    count = lax.axis_size(axes)
    step = 1
    while step < count:
        values = values + lax.ppermute(values, axes, [(i, i ^ step) for i in range(count)])
        step *= 2
    return values


def sum_scatter(values):
    part = lax.psum_scatter(values, "dp", scatter_dimension=0, tiled=True)
    return lax.psum_scatter(part, "expert", scatter_dimension=0, tiled=True)


def lane_padded(parts):
    joined = jnp.concatenate(parts, axis=1)
    return jnp.pad(joined, ((0, 0), (0, -joined.shape[1] % 128)))


def local(
    tokens,
    cotangent,
    lengths,
    routes,
    w_query,
    w_key,
    w_value,
    w_output,
    router,
    gain_first,
    gain_second,
    bias_table,
    w_in,
    w_out,
):
    f32, bf16 = jnp.float32, jnp.bfloat16
    blocks = lengths.shape[0]
    rows, width = tokens.shape
    extent = rows // blocks
    expert_local = w_in.shape[0]
    lanes = lax.axis_size("expert")
    groups = lax.axis_size("dp")
    expert_total = expert_local * lanes
    capacity = 2 * extent // expert_total
    bucket_count = bias_table.shape[0]

    packed = lane_padded(
        (w_query, w_key, w_value, w_output, router, gain_first[:, None], gain_second[:, None])
    )
    dense = lax.all_gather(packed, "expert", axis=0, tiled=True)
    dense = lax.all_gather(dense, "dp", axis=0, tiled=True)
    dense, w_in, w_out = lax.optimization_barrier((dense, w_in, w_out))
    w_in_all = lax.all_gather(w_in, "dp", axis=0, tiled=False)
    w_out_all = lax.all_gather(w_out, "dp", axis=0, tiled=False)
    weight_qkv = dense[:, : 3 * width]
    weight_output = dense[:, 3 * width : 4 * width]
    router_full = dense[:, 4 * width : 4 * width + expert_total]
    gain_one = dense[:, 4 * width + expert_total].astype(f32)
    gain_two = dense[:, 4 * width + expert_total + 1].astype(f32)

    bucket_flat = bucket_grid(extent).reshape(1, extent * extent)
    bucket_hot = (jnp.arange(bucket_count, dtype=jnp.int32)[:, None] == bucket_flat)
    bias_grid = lax.dot_general(
        bias_table,
        bucket_hot.astype(f32),
        (((0,), (0,)), ((), ())),
        precision=lax.Precision.HIGHEST,
        preferred_element_type=f32,
    ).reshape(H, extent, extent)
    allowed = jax.vmap(lambda own: same_sequence(own, extent))(lengths)

    rows_in = tokens.astype(f32)
    scale_one, scaled_one = rms_forward(rows_in, gain_one)
    normed = scaled_one.astype(bf16)
    qkv = jnp.dot(normed, weight_qkv, preferred_element_type=f32).astype(bf16)
    shape = (blocks, extent, H, HD)
    query = qkv[:, :width].reshape(shape)
    key = qkv[:, width : 2 * width].reshape(shape)
    value = qkv[:, 2 * width :].reshape(shape)
    masked = attention_scores(query, key, bias_grid, allowed)
    row_peak = jnp.max(masked, axis=-1, keepdims=True)
    log_total = row_peak + jnp.log(jnp.sum(jnp.exp(masked - row_peak), axis=-1, keepdims=True))
    soft_low = jnp.exp(masked - log_total).astype(bf16)
    context = jnp.einsum("bhpq,bqhd->bphd", soft_low, value, preferred_element_type=f32)
    context = context.reshape(rows, width).astype(bf16)

    middle = rows_in + jnp.dot(context, weight_output, preferred_element_type=f32)
    scale_two, scaled_two = rms_forward(middle, gain_two)
    second = scaled_two.astype(bf16)
    logits = jnp.dot(second, router_full, preferred_element_type=f32)
    exps = jnp.exp(logits - jnp.max(logits, axis=-1, keepdims=True))
    gate_probs = exps / jnp.sum(exps, axis=-1, keepdims=True)
    choose = (routes == jnp.arange(expert_total, dtype=jnp.int32)[None, :]).astype(jnp.int32)
    by_block = choose.reshape(blocks, extent, expert_total)
    slot = jnp.sum(jnp.cumsum(by_block, axis=1) * by_block, axis=-1) - 1
    place = (
        routes[:, 0].reshape(blocks, extent) * (blocks * capacity)
        + jnp.arange(blocks, dtype=jnp.int32)[:, None] * capacity
        + slot
    ).reshape(rows)
    choose_float = choose.astype(f32)
    gate = jnp.sum(gate_probs * choose_float, axis=-1, keepdims=True)
    final = cotangent.astype(f32)
    grad_expert = (gate * final).astype(bf16)

    share = expert_local * blocks * capacity

    def dispatch(values):
        buffer = jnp.zeros((expert_total * blocks * capacity, width), bf16).at[place].set(values)
        got = lax.all_to_all(
            buffer.reshape(lanes, share, width), "expert", split_axis=0, concat_axis=0, tiled=True
        )
        got = got.reshape(lanes, expert_local, blocks * capacity, width)
        return got.transpose(1, 0, 2, 3).reshape(expert_local, lanes * blocks * capacity, width)

    def collect(values):
        sent = values.reshape(expert_local, lanes, blocks * capacity, width).transpose(1, 0, 2, 3)
        got = lax.all_to_all(
            sent.reshape(lanes, share, width), "expert", split_axis=0, concat_axis=0, tiled=True
        )
        return got.reshape(expert_total * blocks * capacity, width)[place].astype(f32)

    expert_rows = dispatch(second)
    grad_rows = dispatch(grad_expert)

    out_total = 0.0
    back_total = 0.0
    hiddens = []
    grad_pres = []
    for group in range(groups):
        pre = jnp.einsum("erd,edf->erf", expert_rows, w_in_all[group], preferred_element_type=f32)
        grad_hidden = jnp.einsum(
            "erd,efd->erf", grad_rows, w_out_all[group], preferred_element_type=f32
        )
        activated, pull = jax.vjp(gelu_tanh, pre)
        hidden = activated.astype(bf16)
        grad_pre = pull(grad_hidden)[0].astype(bf16)
        out_total = out_total + jnp.einsum(
            "erf,efd->erd", hidden, w_out_all[group], preferred_element_type=f32
        )
        back_total = back_total + jnp.einsum(
            "erf,edf->erd", grad_pre, w_in_all[group], preferred_element_type=f32
        )
        hiddens.append(hidden)
        grad_pres.append(grad_pre)
    expert_out = collect(out_total.astype(bf16))
    grad_second = collect(back_total.astype(bf16))
    grad_in_parts = jnp.stack(
        [
            jnp.einsum("erd,erf->edf", expert_rows, own, preferred_element_type=f32).astype(bf16)
            for own in grad_pres
        ]
    )
    grad_in = lax.psum_scatter(grad_in_parts, "dp", scatter_dimension=0, tiled=True)
    grad_out_parts = jnp.stack(
        [
            jnp.einsum("erf,erd->efd", own, grad_rows, preferred_element_type=f32).astype(bf16)
            for own in hiddens
        ]
    )
    grad_out = lax.psum_scatter(grad_out_parts, "dp", scatter_dimension=0, tiled=True)

    block_out = (middle + gate * expert_out).astype(bf16)
    grad_gate = jnp.sum(final * expert_out, axis=-1, keepdims=True)
    grad_logits = (gate_probs * (choose_float * grad_gate - gate * grad_gate)).astype(bf16)
    grad_router = contract_rows(second, grad_logits)
    grad_second = grad_second + contract_cols(grad_logits, router_full)
    grad_part, grad_gain_two = rms_backward(middle, scale_two, gain_two, grad_second)
    grad_middle = final + grad_part
    grad_attended = grad_middle.astype(bf16)
    early = lane_padded(
        (contract_rows(context, grad_attended), grad_router, grad_gain_two[:, None])
    ).astype(bf16)
    early = sum_scatter(early).astype(f32)
    grad_context = contract_cols(grad_attended, weight_output).astype(bf16).reshape(shape)

    soft = jnp.exp(attention_scores(query, key, bias_grid, allowed) - log_total)
    grad_soft = jnp.einsum("bphd,bqhd->bhpq", grad_context, value, preferred_element_type=f32)
    grad_value = jnp.einsum(
        "bhpq,bphd->bqhd", soft.astype(bf16), grad_context, preferred_element_type=f32
    )
    inner = jnp.sum(grad_soft * soft, axis=-1, keepdims=True)
    grad_scores = (soft * (grad_soft - inner)).astype(bf16)
    grad_query = jnp.einsum("bhpq,bqhd->bphd", grad_scores, key, preferred_element_type=f32)
    grad_key = jnp.einsum("bhpq,bphd->bqhd", grad_scores, query, preferred_element_type=f32)
    grad_qkv = jnp.concatenate(
        [
            (grad_query * HD ** (-0.5)).astype(bf16).reshape(rows, width),
            (grad_key * HD ** (-0.5)).astype(bf16).reshape(rows, width),
            grad_value.astype(bf16).reshape(rows, width),
        ],
        axis=1,
    )
    table_rows = jnp.sum(grad_scores.astype(f32), axis=0).astype(bf16)
    grad_table = lax.dot_general(
        bucket_hot.astype(bf16),
        table_rows.reshape(H, extent * extent),
        (((1,), (1,)), ((), ())),
        preferred_element_type=f32,
    )
    grad_table = sum_everywhere(grad_table, ("dp", "expert"))
    grad_normed = contract_cols(grad_qkv, weight_qkv)
    grad_part, grad_gain_one = rms_backward(rows_in, scale_one, gain_one, grad_normed)
    grad_tokens = grad_middle + grad_part
    late = lane_padded((contract_rows(normed, grad_qkv), grad_gain_one[:, None])).astype(bf16)
    late = sum_scatter(late).astype(f32)
    return (
        block_out,
        grad_tokens,
        late[:, :width],
        late[:, width : 2 * width],
        late[:, 2 * width : 3 * width],
        early[:, :width],
        early[:, width : width + expert_total],
        late[:, 3 * width],
        early[:, width + expert_total],
        grad_table,
        grad_in.astype(f32).reshape(w_in.shape),
        grad_out.astype(f32).reshape(w_out.shape),
    )


def solution(mesh):
    placed = (
        P(("dp", "expert"), None),
        P(("dp", "expert"), None),
        P(("dp", "expert"), None),
        P(("dp", "expert"), None),
        P(("dp", "expert"), None),
        P(("dp", "expert"), None),
        P(("dp", "expert"), None),
        P(("dp", "expert"), None),
        P(("dp", "expert"), None),
        P(("dp", "expert")),
        P(("dp", "expert")),
        P(),
        P("expert", None, "dp"),
        P("expert", "dp", None),
    )
    return jax.shard_map(
        local,
        mesh=mesh,
        in_specs=placed,
        out_specs=(
            P(("dp", "expert"), None),
            P(("dp", "expert"), None),
            P(("dp", "expert"), None),
            P(("dp", "expert"), None),
            P(("dp", "expert"), None),
            P(("dp", "expert"), None),
            P(("dp", "expert"), None),
            P(("dp", "expert")),
            P(("dp", "expert")),
            P(),
            P("expert", None, "dp"),
            P("expert", "dp", None),
        ),
        check_vma=False,
    )
```

```python
import jax
import jax.numpy as jnp
from jax import lax
from jax.experimental import pallas as pl
from jax.experimental.pallas import tpu as pltpu
from jax.sharding import PartitionSpec as P

H = 12
HD = 64


EPSILON = 1e-06
THRESHOLDS = (12, 16, 23, 32, 46, 64, 91)
NEGATIVE = -1e30


def bucket_grid(extent):
    places = jnp.arange(extent, dtype=jnp.int32)
    offset = places[None, :] - places[:, None]
    spread = jnp.abs(offset)
    beyond = 8 + sum(((spread >= threshold).astype(jnp.int32) for threshold in THRESHOLDS))
    return jnp.where(offset > 0, 16, 0).astype(jnp.int32) + jnp.where(spread < 8, spread, beyond)


def same_sequence(seq_lengths, extent):
    places = jnp.arange(extent, dtype=jnp.int32)
    ending = jnp.cumsum(seq_lengths)
    segment = jnp.sum((places[:, None] >= ending[None, :]).astype(jnp.int32), axis=1)
    return segment[:, None] == segment[None, :]


def gelu_tanh(values):
    return jax.nn.gelu(values, approximate=True)


def rms_forward(values, gain_vector):
    scale_row = lax.rsqrt(jnp.mean(values * values, axis=-1, keepdims=True) + EPSILON)
    return (scale_row, values * scale_row * gain_vector)


def rms_backward(values, scale_row, gain_vector, grad_scaled):
    weighted = grad_scaled * gain_vector
    grad_values = scale_row * weighted - values * scale_row**3 * jnp.mean(
        weighted * values, axis=-1, keepdims=True
    )
    grad_gain = jnp.sum(grad_scaled * values * scale_row, axis=0)
    return (grad_values, grad_gain)


def contract_rows(former, latter):
    return lax.dot_general(
        former, latter, (((0,), (0,)), ((), ())), preferred_element_type=jnp.float32
    )


def contract_cols(former, latter):
    return lax.dot_general(
        former, latter, (((1,), (1,)), ((), ())), preferred_element_type=jnp.float32
    )


def bias_kernel(line_ref, grid_ref):
    extent = grid_ref.shape[1]
    wide = jnp.broadcast_to(line_ref[0], (extent, 2 * extent))
    turned = pltpu.roll(wide, extent + 1, 1, stride=1, stride_axis=0)
    grid_ref[0] = turned[:, :extent]


def bias_of_offsets(bias_table, extent):
    offset = jnp.arange(2 * extent, dtype=jnp.int32) - (extent - 1)
    spread = jnp.abs(offset)
    beyond = 8 + sum(((spread >= threshold).astype(jnp.int32) for threshold in THRESHOLDS))
    bucket = jnp.where(offset > 0, 16, 0) + jnp.where(spread < 8, spread, beyond)
    hot = (jnp.arange(bias_table.shape[0], dtype=jnp.int32)[:, None] == bucket[None, :])
    line = jnp.sum(bias_table[:, :, None] * hot.astype(jnp.float32)[:, None, :], axis=0)
    return pl.pallas_call(
        bias_kernel,
        grid=(H,),
        in_specs=[pl.BlockSpec((1, 1, 2 * extent), lambda h: (h, 0, 0))],
        out_specs=pl.BlockSpec((1, extent, extent), lambda h: (h, 0, 0)),
        out_shape=jax.ShapeDtypeStruct((H, extent, extent), jnp.float32),
        compiler_params=pltpu.CompilerParams(vmem_limit_bytes=32 * 1024 * 1024),
        name="bias_grid",
    )(line[:, None, :])


def attention_scores(query, key, bias_grid, allowed):
    scores = jnp.einsum("bphd,bqhd->bhpq", query, key, preferred_element_type=jnp.float32)
    return jnp.where(allowed[:, None], scores * HD ** (-0.5) + bias_grid[None], NEGATIVE)


def sum_everywhere(values, axes):
    count = lax.axis_size(axes)
    step = 1
    while step < count:
        values = values + lax.ppermute(values, axes, [(i, i ^ step) for i in range(count)])
        step *= 2
    return values


def sum_scatter(values):
    part = lax.psum_scatter(values, "dp", scatter_dimension=0, tiled=True)
    return lax.psum_scatter(part, "expert", scatter_dimension=0, tiled=True)


def lane_padded(parts):
    joined = jnp.concatenate(parts, axis=1)
    return jnp.pad(joined, ((0, 0), (0, -joined.shape[1] % 128)))


def local(
    tokens,
    cotangent,
    lengths,
    routes,
    w_query,
    w_key,
    w_value,
    w_output,
    router,
    gain_first,
    gain_second,
    bias_table,
    w_in,
    w_out,
):
    f32, bf16 = jnp.float32, jnp.bfloat16
    blocks = lengths.shape[0]
    rows, width = tokens.shape
    extent = rows // blocks
    expert_local = w_in.shape[0]
    lanes = lax.axis_size("expert")
    groups = lax.axis_size("dp")
    expert_total = expert_local * lanes
    capacity = 2 * extent // expert_total
    bucket_count = bias_table.shape[0]

    packed = lane_padded(
        (w_query, w_key, w_value, w_output, router, gain_first[:, None], gain_second[:, None])
    )
    dense = lax.all_gather(packed, "expert", axis=0, tiled=True)
    dense = lax.all_gather(dense, "dp", axis=0, tiled=True)
    dense, w_in, w_out = lax.optimization_barrier((dense, w_in, w_out))
    w_in_all = lax.all_gather(w_in, "dp", axis=0, tiled=False)
    w_out_all = lax.all_gather(w_out, "dp", axis=0, tiled=False)
    bucket_flat = bucket_grid(extent).reshape(1, extent * extent)
    bucket_hot = (jnp.arange(bucket_count, dtype=jnp.int32)[:, None] == bucket_flat)
    bias_grid = bias_of_offsets(bias_table, extent)
    choose = (routes == jnp.arange(expert_total, dtype=jnp.int32)[None, :]).astype(jnp.int32)
    by_block = choose.reshape(blocks, extent, expert_total)
    slot = jnp.sum(jnp.cumsum(by_block, axis=1) * by_block, axis=-1) - 1
    place = (
        routes[:, 0].reshape(blocks, extent) * (blocks * capacity)
        + jnp.arange(blocks, dtype=jnp.int32)[:, None] * capacity
        + slot
    ).reshape(rows)

    share = expert_local * blocks * capacity

    def dispatch(values):
        buffer = jnp.zeros((expert_total * blocks * capacity, width), bf16).at[place].set(values)
        got = lax.all_to_all(
            buffer.reshape(lanes, share, width), "expert", split_axis=0, concat_axis=0, tiled=True
        )
        got = got.reshape(lanes, expert_local, blocks * capacity, width)
        return got.transpose(1, 0, 2, 3).reshape(expert_local, lanes * blocks * capacity, width)

    gained_rows = dispatch(cotangent)
    dense, bias_grid, gained_rows = lax.optimization_barrier((dense, bias_grid, gained_rows))
    weight_qkv = dense[:, : 3 * width]
    weight_output = dense[:, 3 * width : 4 * width]
    router_full = dense[:, 4 * width : 4 * width + expert_total]
    gain_one = dense[:, 4 * width + expert_total].astype(f32)
    gain_two = dense[:, 4 * width + expert_total + 1].astype(f32)
    allowed = jax.vmap(lambda own: same_sequence(own, extent))(lengths)

    rows_in = tokens.astype(f32)
    scale_one, scaled_one = rms_forward(rows_in, gain_one)
    normed = scaled_one.astype(bf16)
    qkv = jnp.dot(normed, weight_qkv, preferred_element_type=f32).astype(bf16)
    shape = (blocks, extent, H, HD)
    query = qkv[:, :width].reshape(shape)
    key = qkv[:, width : 2 * width].reshape(shape)
    value = qkv[:, 2 * width :].reshape(shape)
    masked = attention_scores(query, key, bias_grid, allowed)
    row_peak = jnp.max(masked, axis=-1, keepdims=True)
    log_total = row_peak + jnp.log(jnp.sum(jnp.exp(masked - row_peak), axis=-1, keepdims=True))
    soft_low = jnp.exp(masked - log_total).astype(bf16)
    context = jnp.einsum("bhpq,bqhd->bphd", soft_low, value, preferred_element_type=f32)
    context = context.reshape(rows, width).astype(bf16)

    middle = rows_in + jnp.dot(context, weight_output, preferred_element_type=f32)
    scale_two, scaled_two = rms_forward(middle, gain_two)
    second = scaled_two.astype(bf16)
    logits = jnp.dot(second, router_full, preferred_element_type=f32)
    exps = jnp.exp(logits - jnp.max(logits, axis=-1, keepdims=True))
    gate_probs = exps / jnp.sum(exps, axis=-1, keepdims=True)
    choose_float = choose.astype(f32)
    gate = jnp.sum(gate_probs * choose_float, axis=-1, keepdims=True)
    final = cotangent.astype(f32)
    def collect_start(values):
        sent = values.reshape(expert_local, lanes, blocks * capacity, width).transpose(1, 0, 2, 3)
        got = lax.all_to_all(
            sent.reshape(lanes, share, width), "expert", split_axis=0, concat_axis=0, tiled=True
        )
        return got.reshape(expert_total * blocks * capacity, width)

    def collect(values):
        return collect_start(values)[place].astype(f32)

    expert_rows = dispatch(second)
    gained = gained_rows.astype(f32)
    row_logits = jnp.einsum("erd,dk->erk", expert_rows, router_full, preferred_element_type=f32)
    row_exps = jnp.exp(row_logits - jnp.max(row_logits, axis=-1, keepdims=True))
    row_probs = row_exps / jnp.sum(row_exps, axis=-1, keepdims=True)
    own_expert = lax.axis_index("expert") * expert_local + jnp.arange(expert_local, dtype=jnp.int32)
    own_hot = (own_expert[:, None] == jnp.arange(expert_total, dtype=jnp.int32)[None, :])
    own_hot = own_hot.astype(f32)[:, None, :]
    row_gate = jnp.sum(row_probs * own_hot, axis=-1, keepdims=True)
    grad_rows = (row_gate * gained).astype(bf16)

    pres = []
    hiddens = []
    for group in range(groups):
        pre = jnp.einsum("erd,edf->erf", expert_rows, w_in_all[group], preferred_element_type=f32)
        pres.append(pre)
        hiddens.append(gelu_tanh(pre).astype(bf16))
    grad_out_parts = jnp.stack(
        [
            jnp.einsum("erf,erd->efd", own, grad_rows, preferred_element_type=f32).astype(bf16)
            for own in hiddens
        ]
    )
    grad_out_parts, hiddens = lax.optimization_barrier((grad_out_parts, hiddens))
    grad_out = lax.psum_scatter(grad_out_parts, "dp", scatter_dimension=0, tiled=True)
    out_total = 0.0
    for group in range(groups):
        out_total = out_total + jnp.einsum(
            "erf,efd->erd", hiddens[group], w_out_all[group], preferred_element_type=f32
        )
    out_low = out_total.astype(bf16)
    expert_out = collect(out_low)
    row_grad_gate = jnp.sum(gained * out_low.astype(f32), axis=-1, keepdims=True)
    grad_logits = (row_probs * (own_hot * row_grad_gate - row_gate * row_grad_gate)).astype(bf16)
    grad_router = jnp.einsum("erd,erk->dk", expert_rows, grad_logits, preferred_element_type=f32)
    back_total = jnp.einsum("erk,dk->erd", grad_logits, router_full, preferred_element_type=f32)
    grad_pres = []
    for group in range(groups):
        grad_hidden = jnp.einsum(
            "erd,efd->erf", grad_rows, w_out_all[group], preferred_element_type=f32
        )
        grad_pre = jax.vjp(gelu_tanh, pres[group])[1](grad_hidden)[0].astype(bf16)
        back_total = back_total + jnp.einsum(
            "erf,edf->erd", grad_pre, w_in_all[group], preferred_element_type=f32
        )
        grad_pres.append(grad_pre)
    back_low = collect_start(back_total.astype(bf16))
    grad_in_parts = jnp.stack(
        [
            jnp.einsum("erd,erf->edf", expert_rows, own, preferred_element_type=f32).astype(bf16)
            for own in grad_pres
        ]
    )
    back_low, grad_in_parts = lax.optimization_barrier((back_low, grad_in_parts))
    grad_in = lax.psum_scatter(grad_in_parts, "dp", scatter_dimension=0, tiled=True)
    grad_second = back_low[place].astype(f32)

    block_out = (middle + gate * expert_out).astype(bf16)
    grad_part, grad_gain_two = rms_backward(middle, scale_two, gain_two, grad_second)
    grad_middle = final + grad_part
    grad_attended = grad_middle.astype(bf16)
    grad_context = contract_cols(grad_attended, weight_output).astype(bf16).reshape(shape)

    soft = jnp.exp(attention_scores(query, key, bias_grid, allowed) - log_total)
    grad_soft = jnp.einsum("bphd,bqhd->bhpq", grad_context, value, preferred_element_type=f32)
    grad_value = jnp.einsum(
        "bhpq,bphd->bqhd", soft.astype(bf16), grad_context, preferred_element_type=f32
    )
    inner = jnp.sum(grad_soft * soft, axis=-1, keepdims=True)
    grad_scores = (soft * (grad_soft - inner)).astype(bf16)
    grad_query = jnp.einsum("bhpq,bqhd->bphd", grad_scores, key, preferred_element_type=f32)
    grad_key = jnp.einsum("bhpq,bphd->bqhd", grad_scores, query, preferred_element_type=f32)
    grad_qkv = jnp.concatenate(
        [
            (grad_query * HD ** (-0.5)).astype(bf16).reshape(rows, width),
            (grad_key * HD ** (-0.5)).astype(bf16).reshape(rows, width),
            grad_value.astype(bf16).reshape(rows, width),
        ],
        axis=1,
    )
    table_rows = jnp.sum(grad_scores.astype(f32), axis=0).astype(bf16)
    grad_table = lax.dot_general(
        bucket_hot.astype(bf16),
        table_rows.reshape(H, extent * extent),
        (((1,), (1,)), ((), ())),
        preferred_element_type=f32,
    )
    grad_table = sum_everywhere(grad_table, ("dp", "expert"))
    grad_normed = contract_cols(grad_qkv, weight_qkv)
    grad_part, grad_gain_one = rms_backward(rows_in, scale_one, gain_one, grad_normed)
    grad_tokens = grad_middle + grad_part
    sums = lane_padded(
        (
            contract_rows(normed, grad_qkv),
            contract_rows(context, grad_attended),
            grad_router,
            grad_gain_one[:, None],
            grad_gain_two[:, None],
        )
    ).astype(bf16)
    sums = sum_scatter(sums).astype(f32)
    return (
        block_out,
        grad_tokens,
        sums[:, :width],
        sums[:, width : 2 * width],
        sums[:, 2 * width : 3 * width],
        sums[:, 3 * width : 4 * width],
        sums[:, 4 * width : 4 * width + expert_total],
        sums[:, 4 * width + expert_total],
        sums[:, 4 * width + expert_total + 1],
        grad_table,
        grad_in.astype(f32).reshape(w_in.shape),
        grad_out.astype(f32).reshape(w_out.shape),
    )


def solution(mesh):
    placed = (
        P(("dp", "expert"), None),
        P(("dp", "expert"), None),
        P(("dp", "expert"), None),
        P(("dp", "expert"), None),
        P(("dp", "expert"), None),
        P(("dp", "expert"), None),
        P(("dp", "expert"), None),
        P(("dp", "expert"), None),
        P(("dp", "expert"), None),
        P(("dp", "expert")),
        P(("dp", "expert")),
        P(),
        P("expert", None, "dp"),
        P("expert", "dp", None),
    )
    return jax.shard_map(
        local,
        mesh=mesh,
        in_specs=placed,
        out_specs=(
            P(("dp", "expert"), None),
            P(("dp", "expert"), None),
            P(("dp", "expert"), None),
            P(("dp", "expert"), None),
            P(("dp", "expert"), None),
            P(("dp", "expert"), None),
            P(("dp", "expert"), None),
            P(("dp", "expert")),
            P(("dp", "expert")),
            P(),
            P("expert", None, "dp"),
            P("expert", "dp", None),
        ),
        check_vma=False,
    )
```
